32 devices in a mesh: shard: 4 (over y, x), ctx: 4 (over z), tp: 2 (over core).
Axes of the slice: x: 2, y: 2, z: 4, core: 2. Of those that a mesh axis runs over, the one named last changes fastest.
Arguments:
- hidden_in: bfloat16 [8192, 1024], P(('shard', 'ctx')), may hold values from -6 to 6
- cotangent: bfloat16 [8192, 1024], P(('shard', 'ctx')), may hold values from -6 to 6
- lengths: int32 [4, 3], P('shard'), may hold values from 1 to 1536, as said below
- first_gain: bfloat16 [1024], P(('shard', 'ctx')), may hold values from 0.5 to 1.5
- second_gain: bfloat16 [1024], P(('shard', 'ctx')), may hold values from 0.25 to 1.75
- mamba_gate: bfloat16 [1024, 1536], P(('shard', 'ctx'), 'tp'), may hold values from -0.1875 to 0.1875
- mamba_inner: bfloat16 [1024, 1536], P(('shard', 'ctx'), 'tp'), may hold values from -0.1875 to 0.1875
- mamba_step: bfloat16 [1024, 24], P(('shard', 'ctx'), 'tp'), may hold values from -0.1875 to 0.1875
- mamba_states: bfloat16 [1024, 256], P(('shard', 'ctx')), may hold values from -0.09375 to 0.09375
- query_weight: bfloat16 [1024, 512], P(('shard', 'ctx'), 'tp'), may hold values from -0.1875 to 0.1875
- keyval_weight: bfloat16 [1024, 256], P(('shard', 'ctx'), 'tp'), may hold values from -0.1875 to 0.1875
- mamba_output: bfloat16 [1536, 1024], P('tp', ('shard', 'ctx')), may hold values from -0.15625 to 0.15625
- attention_output: bfloat16 [512, 1024], P('tp', ('shard', 'ctx')), may hold values from -1 to 1
- gate_weight: bfloat16 [1024, 2048], P(('shard', 'ctx'), 'tp'), may hold values from -0.1875 to 0.1875
- up_weight: bfloat16 [1024, 2048], P(('shard', 'ctx'), 'tp'), may hold values from -0.1875 to 0.1875
- down_weight: bfloat16 [2048, 1024], P('tp', ('shard', 'ctx')), may hold values from -0.125 to 0.125
- decay_log: float32 [24], P('tp'), may hold values from -9 to 0
- step_bias: float32 [24], P('tp'), may hold values from -4.5 to -2
- skip_gain: float32 [24], P('tp'), may hold values from 0.5 to 1.5
- conv_inner: bfloat16 [4, 1536], P(None, 'tp'), may hold values from -3 to 3
- conv_inner_bias: bfloat16 [1536], P('tp'), may hold values from -0.5 to 0.5
- conv_states: bfloat16 [4, 256], replicated, may hold values from -3 to 3
- conv_states_bias: bfloat16 [256], replicated, may hold values from -0.19921875 to 0.19921875
Outputs:
- output: float32 [8192, 1024], P(('shard', 'ctx'))
- grad_input: float32 [8192, 1024], P(('shard', 'ctx'))
- grad_first_gain: float32 [1024], P(('shard', 'ctx'))
- grad_second_gain: float32 [1024], P(('shard', 'ctx'))
- grad_mamba_gate: float32 [1024, 1536], P(('shard', 'ctx'), 'tp')
- grad_mamba_inner: float32 [1024, 1536], P(('shard', 'ctx'), 'tp')
- grad_mamba_step: float32 [1024, 24], P(('shard', 'ctx'), 'tp')
- grad_mamba_states: float32 [1024, 256], P(('shard', 'ctx'))
- grad_query_weight: float32 [1024, 512], P(('shard', 'ctx'), 'tp')
- grad_keyval_weight: float32 [1024, 256], P(('shard', 'ctx'), 'tp')
- grad_mamba_output: float32 [1536, 1024], P('tp', ('shard', 'ctx'))
- grad_attention_output: float32 [512, 1024], P('tp', ('shard', 'ctx'))
- grad_gate_weight: float32 [1024, 2048], P(('shard', 'ctx'), 'tp')
- grad_up_weight: float32 [1024, 2048], P(('shard', 'ctx'), 'tp')
- grad_down_weight: float32 [2048, 1024], P('tp', ('shard', 'ctx'))
- grad_decay_log: float32 [24], P('tp')
- grad_step_bias: float32 [24], P('tp')
- grad_skip_gain: float32 [24], P('tp')
- grad_conv_inner: float32 [4, 1536], P(None, 'tp')
- grad_conv_inner_bias: float32 [1536], P('tp')
- grad_conv_states: float32 [4, 256], replicated
- grad_conv_states_bias: float32 [256], replicated
The draws below stay inside these ranges and needn't reach their ends.
Inputs may be any that keep to these rules, and one draw needn't show every extreme that they name: `lengths`: in each group the first and the last document lie inside one span of 256 positions each, the middle one fills the 6 spans between them completely; every document starts at a multiple of 256.
All inputs are finite; a program needn't handle non-finite values.
Results may differ from the reference program's by a relative error of at most 0.04.
Values may be sent and summed in bfloat16 or wider, within the bound.
A program may use at most 192 MiB of HBM per device.

```python
import jax
import jax.numpy as jnp
from jax import lax

D = 1024
HEADS_M = 24
HEAD_DIM = 64
STATE = 128
QH = 8
KVH = 2
FF = 2048
SPAN = 256
CONV = 4
DOCS = 3
T_DEV = 512
SPANS = 8
TOKENS = 8192
MAMBA_W = 1536
Q_W = 512
KV_W = 256
N_SHARD = 4
N_CTX = 4


def draw_lengths(key, part):
    key = jax.random.fold_in(key, 11)
    ragged = jax.random.randint(key, (N_SHARD, 2), 1, SPAN + 1, dtype=jnp.int32)
    middle = jnp.full((N_SHARD, 1), (SPANS - 2) * SPAN, jnp.int32)
    return jnp.concatenate([ragged[:, :1], middle, ragged[:, 1:]], axis=1)


def block_scale(rng, shape, cuts, least, largest):
    def one(dim, parts):
        draws = jax.random.uniform(jax.random.fold_in(jax.random.fold_in(rng, 6), dim), (parts,), jnp.float32, least / len(cuts), largest / len(cuts))
        return jnp.repeat(jnp.exp(draws), shape[dim] // parts).reshape((-1,) + (1,) * (len(shape) - dim - 1))

    loudness = one(*cuts[0])
    for cut in cuts[1:]:
        loudness = loudness * one(*cut)
    return loudness


def normal_values(rng, dims, spread, limit, cuts=(), kind=jnp.bfloat16):
    values = jax.random.normal(rng, dims, jnp.float32) * spread
    if len(cuts) > 0:
        values = block_scale(rng, dims, cuts, -0.22, 0.18) * values
    return jnp.clip(values, min=-limit, max=limit).astype(kind)


def setup_inputs(seed: int = 0) -> dict:
    keys = jax.random.split(jax.random.key(seed), 24)
    return {
        "hidden_in": normal_values(keys[0], (TOKENS, D), 1.0, 6.0, ((0, 16),)),
        "cotangent": normal_values(keys[1], (TOKENS, D), 1.0, 6.0, ((0, 16),)),
        "lengths": draw_lengths(jax.random.fold_in(keys[23], 71), 0),
        "first_gain": jnp.clip(1.0 + 0.1 * jax.random.normal(keys[3], (D,), jnp.float32), 0.5, 1.5).astype(jnp.bfloat16),
        "second_gain": jnp.clip(1.0 + 0.15 * jax.random.normal(keys[4], (D,), jnp.float32), 0.25, 1.75).astype(jnp.bfloat16),
        "mamba_gate": normal_values(keys[5], (D, MAMBA_W), D ** -0.5, 0.1875, ((0, 16), (1, 2))),
        "mamba_inner": normal_values(keys[6], (D, MAMBA_W), D ** -0.5, 0.1875, ((0, 16), (1, 2))),
        "mamba_step": normal_values(keys[7], (D, HEADS_M), D ** -0.5, 0.1875, ((0, 16), (1, 2))),
        "mamba_states": normal_values(keys[8], (D, 2 * STATE), (4 * D) ** -0.5, 0.09375, ((0, 16),)),
        "query_weight": normal_values(keys[9], (D, Q_W), D ** -0.5, 0.1875, ((0, 16), (1, 2))),
        "keyval_weight": normal_values(keys[10], (D, KV_W), D ** -0.5, 0.1875, ((0, 16), (1, 2))),
        "mamba_output": normal_values(keys[11], (MAMBA_W, D), MAMBA_W ** -0.5, 0.15625, ((0, 2), (1, 16))),
        "attention_output": normal_values(keys[12], (Q_W, D), (Q_W // 16) ** -0.5, 1.0, ((0, 2), (1, 16))),
        "gate_weight": normal_values(keys[13], (D, FF), D ** -0.5, 0.1875, ((0, 16), (1, 2))),
        "up_weight": normal_values(keys[14], (D, FF), D ** -0.5, 0.1875, ((0, 16), (1, 2))),
        "down_weight": normal_values(keys[15], (FF, D), FF ** -0.5, 0.125, ((0, 2), (1, 16))),
        "decay_log": jnp.clip(-9.0 + 9.0 * jax.random.uniform(keys[16], (HEADS_M,), jnp.float32) ** block_scale(keys[16], (HEADS_M,), ((0, 2),), -0.2, 0.2), -9.0, 0.0),
        "step_bias": jnp.clip(-4.5 + 2.5 * jax.random.uniform(keys[17], (HEADS_M,), jnp.float32) ** block_scale(keys[17], (HEADS_M,), ((0, 2),), -0.2, 0.2), -4.5, -2.0),
        "skip_gain": jnp.clip(0.5 + 1.0 * jax.random.uniform(keys[18], (HEADS_M,), jnp.float32) ** block_scale(keys[18], (HEADS_M,), ((0, 2),), -0.2, 0.2), 0.5, 1.5),
        "conv_inner": normal_values(keys[19], (CONV, MAMBA_W), CONV ** -0.5, 3.0, ((1, 2),)),
        "conv_inner_bias": jnp.clip(jax.random.uniform(keys[20], (MAMBA_W,), jnp.float32, -0.5, 0.5) * block_scale(keys[20], (MAMBA_W,), ((0, 2),), -0.4, 0.0), -0.5, 0.5).astype(jnp.bfloat16),
        "conv_states": normal_values(keys[21], (CONV, 2 * STATE), CONV ** -0.5, 3.0),
        "conv_states_bias": jnp.clip(jax.random.uniform(keys[22], (2 * STATE,), jnp.float32, -0.19921875, 0.19921875), -0.19921875, 0.19921875).astype(jnp.bfloat16),
    }


@jax.custom_vjp
def low(v):
    return lax.optimization_barrier(v.astype(jnp.bfloat16)).astype(jnp.float32)

@jax.custom_vjp
def low_back(v):
    return v

def low_keep(v):
    return (low(v), None)

def low_pass(kept, grad):
    return (grad,)

def back_keep(v):
    return (v, None)

def back_low(kept, grad):
    return (low(grad),)
low.defvjp(low_keep, low_pass)
low_back.defvjp(back_keep, back_low)
HIGHEST_PREC = lax.Precision.HIGHEST
NORM_EPS = 1e-05
MASK_FILL = -1e+30

def token_layout(seq_lens, first_row, row_count):
    span_counts = (seq_lens + SPAN - 1) // SPAN
    span_begin = jnp.cumsum(span_counts, dtype=jnp.int32) - span_counts
    row_index = first_row + jnp.arange(row_count, dtype=jnp.int32)
    row_span = row_index // SPAN
    row_doc = lax.optimization_barrier(jnp.sum((row_span[:, None] >= span_begin[None, 1:]).astype(jnp.int32), axis=1, dtype=jnp.int32))
    doc_onehot = row_doc[:, None] == jnp.arange(DOCS, dtype=jnp.int32)[None, :]
    doc_start = lax.optimization_barrier(jnp.sum(jnp.where(doc_onehot, span_begin[None, :], 0), axis=1, dtype=jnp.int32)) * SPAN
    doc_length = lax.optimization_barrier(jnp.sum(jnp.where(doc_onehot, seq_lens[None, :], 0), axis=1, dtype=jnp.int32))
    row_pos = row_index - doc_start
    return (row_index, row_doc, row_pos, row_pos < doc_length)

def apply_rotary(values, positions, direction):
    half_dim = values.shape[-1] // 2
    frequency = 10000.0 ** (-jnp.arange(half_dim, dtype=jnp.float32) / half_dim)
    angles = positions.astype(jnp.float32)[:, None] * frequency[None, :]
    cosine = jnp.cos(angles)[:, None, :]
    sine_dir = direction * jnp.sin(angles)[:, None, :]
    leading = values[..., :half_dim]
    trailing = values[..., half_dim:]
    return jnp.concatenate([leading * cosine - trailing * sine_dir, leading * sine_dir + trailing * cosine], axis=-1)

def rms_scale(values, gain_vec):
    return values * lax.rsqrt(lax.optimization_barrier(jnp.mean(values * values, axis=-1, keepdims=True)) + NORM_EPS) * gain_vec

def causal_conv(values, kernel, bias, positions):
    row_count = values.shape[0]
    total = bias[None, :] + jnp.zeros_like(values)
    for tap_no in range(CONV):
        lag = CONV - 1 - tap_no
        if lag > 0:
            moved = jnp.concatenate([jnp.zeros((lag, values.shape[1]), values.dtype), values[:row_count - lag]], axis=0)
        else:
            moved = values
        keep = (positions >= lag).astype(jnp.float32)[:, None]
        total = total + kernel[tap_no][None, :] * moved * keep
    return total

def attention_group(query_rot, key_rot, value_low, row_doc, row_valid):
    group_rows = query_rot.shape[0]
    block_rows = min(512, group_rows)
    key_index = jnp.arange(group_rows, dtype=jnp.int32)
    scale_factor = HEAD_DIM ** (-0.5)

    def one_block(block_no):
        begin = block_no * block_rows
        query_block = lax.dynamic_slice_in_dim(query_rot, begin, block_rows, 0)
        query_doc = lax.dynamic_slice_in_dim(row_doc, begin, block_rows, 0)
        query_index = begin + jnp.arange(block_rows, dtype=jnp.int32)
        scores = low_back(jnp.einsum('bgrd,kgd->bgrk', query_block, key_rot, precision=HIGHEST_PREC) * scale_factor)
        allowed = (query_doc[:, None] == row_doc[None, :]) & (key_index[None, :] <= query_index[:, None]) & row_valid[None, :]
        scores = jnp.where(allowed[:, None, None, :], scores, MASK_FILL)
        probs = jax.nn.softmax(scores, axis=-1)
        return jnp.einsum('bgrk,kgd->bgrd', low(probs), value_low, precision=HIGHEST_PREC)
    blocks = lax.map(jax.checkpoint(one_block), jnp.arange(group_rows // block_rows, dtype=jnp.int32))
    return blocks.reshape(group_rows, -1)

def mamba_span(carried, inputs):
    inner_c, b_mat, c_mat, step_c, decay_c, span_flag = inputs
    cumul = jnp.cumsum(decay_c, axis=0)
    carried = carried * span_flag
    inflow = jnp.exp(cumul)[:, :, None] * jnp.einsum('qn,hnp->qhp', c_mat, carried, precision=HIGHEST_PREC)
    lower = jnp.arange(SPAN)[:, None] >= jnp.arange(SPAN)[None, :]
    gaps = cumul[:, None, :] - cumul[None, :, :]
    decay_mat = jnp.exp(jnp.where(lower[:, :, None], gaps, MASK_FILL))
    intersection = jnp.dot(c_mat, b_mat.T, precision=HIGHEST_PREC)
    mixing = decay_mat * intersection[:, :, None] * step_c[None, :, :]
    within = jnp.einsum('qkh,khp->qhp', mixing, inner_c, precision=HIGHEST_PREC)
    span_tail = cumul[-1]
    weights_in = jnp.exp(span_tail[None, :] - cumul) * step_c
    carried = jnp.exp(span_tail)[:, None, None] * carried + jnp.einsum('qh,qn,qhp->hnp', weights_in, b_mat, inner_c, precision=HIGHEST_PREC)
    return (carried, inflow + within)

def group_forward(hidden, seq_lens, params):
    gain_one, gain_two, mgate_w, inner_w, step_w, states_w, query_w, keyval_w, mout_w, aout_w, gate_w, upper_w, down_w, decay_log, step_bias, skip_gain, conv_in_w, conv_in_b, conv_st_w, conv_st_b = params
    group_rows = hidden.shape[0]
    row_index, row_doc, row_pos, row_valid = token_layout(seq_lens, 0, group_rows)
    mixer_in = low(rms_scale(hidden, gain_one))
    query_lin = low_back(jnp.dot(mixer_in, query_w, precision=HIGHEST_PREC)).reshape(group_rows, QH, HEAD_DIM)
    keyval_lin = low_back(jnp.dot(mixer_in, keyval_w, precision=HIGHEST_PREC)).reshape(group_rows, KVH, 2, HEAD_DIM)
    query_rot = low(apply_rotary(query_lin, row_pos, 1.0)).reshape(group_rows, KVH, QH // KVH, HEAD_DIM)
    key_rot = low(apply_rotary(keyval_lin[:, :, 0], row_pos, 1.0))
    value_low = low(keyval_lin[:, :, 1])
    attn_heads = low(low_back(attention_group(query_rot, key_rot, value_low, row_doc, row_valid)))
    attn_part = jnp.dot(attn_heads, aout_w, precision=HIGHEST_PREC)
    mgate_lin = low_back(jnp.dot(mixer_in, mgate_w, precision=HIGHEST_PREC))
    inner_pre = low(low_back(jnp.dot(mixer_in, inner_w, precision=HIGHEST_PREC)))
    states_pre = low(low_back(jnp.dot(mixer_in, states_w, precision=HIGHEST_PREC)))
    inner_low = low(jax.nn.silu(causal_conv(inner_pre, conv_in_w, conv_in_b, row_pos)))
    states_low = low(jax.nn.silu(causal_conv(states_pre, conv_st_w, conv_st_b, row_pos)))
    step_raw = low_back(jnp.dot(mixer_in, step_w, precision=HIGHEST_PREC))
    step_size = jax.nn.softplus(step_raw + step_bias[None, :]) * row_valid.astype(jnp.float32)[:, None]
    log_decay = -jnp.exp(decay_log)[None, :] * step_size
    span_flag = (row_pos[::SPAN] != 0).astype(jnp.float32)
    span_total = group_rows // SPAN
    inner_heads = inner_low.reshape(group_rows, HEADS_M, HEAD_DIM)
    scan_inputs = (inner_heads.reshape(span_total, SPAN, HEADS_M, HEAD_DIM), states_low[:, :STATE].reshape(span_total, SPAN, STATE), states_low[:, STATE:].reshape(span_total, SPAN, STATE), step_size.reshape(span_total, SPAN, HEADS_M), log_decay.reshape(span_total, SPAN, HEADS_M), span_flag)
    start_state = jnp.zeros((HEADS_M, STATE, HEAD_DIM), jnp.float32)
    _, mamba_y = lax.scan(jax.checkpoint(mamba_span), start_state, scan_inputs)
    mamba_y = mamba_y.reshape(group_rows, HEADS_M, HEAD_DIM) + skip_gain[None, :, None] * inner_heads
    gated_low = low(mamba_y.reshape(group_rows, -1) * jax.nn.silu(mgate_lin))
    mamba_part = jnp.dot(gated_low, mout_w, precision=HIGHEST_PREC)
    resid = hidden + low_back(attn_part + mamba_part)
    ffn_in = low(rms_scale(resid, gain_two))
    gate_lin = low_back(jnp.dot(ffn_in, gate_w, precision=HIGHEST_PREC))
    upper_lin = low_back(jnp.dot(ffn_in, upper_w, precision=HIGHEST_PREC))
    act_low = low(jax.nn.silu(gate_lin) * upper_lin)
    return resid + jnp.dot(act_low, down_w, precision=HIGHEST_PREC)

def reference(hidden_in, cotangent, lengths, first_gain, second_gain, mamba_gate, mamba_inner, mamba_step, mamba_states, query_weight, keyval_weight, mamba_output, attention_output, gate_weight, up_weight, down_weight, decay_log, step_bias, skip_gain, conv_inner, conv_inner_bias, conv_states, conv_states_bias):
    params = tuple((item.astype(jnp.float32) for item in (first_gain, second_gain, mamba_gate, mamba_inner, mamba_step, mamba_states, query_weight, keyval_weight, mamba_output, attention_output, gate_weight, up_weight, down_weight, decay_log, step_bias, skip_gain, conv_inner, conv_inner_bias, conv_states, conv_states_bias)))
    hidden_f = hidden_in.astype(jnp.float32)
    group_rows = T_DEV * N_CTX

    def forward(hidden, weights):
        pieces = []
        for group_no in range(N_SHARD):
            part_rows = hidden[group_no * group_rows:(group_no + 1) * group_rows]
            pieces.append(jax.checkpoint(group_forward)(part_rows, lengths[group_no], weights))
        return jnp.concatenate(pieces, axis=0)
    result, pullback = jax.vjp(forward, hidden_f, params)
    grad_hidden, grad_params = pullback(cotangent.astype(jnp.float32))
    return (result, grad_hidden) + tuple(grad_params)
```

```python
import jax
import jax.numpy as jnp
from jax import lax
from jax.sharding import PartitionSpec as P

HEAD_DIM = 64
STATE = 128
SPAN = 256
CONV = 4
DOCS = 3


NORM_EPS = 1e-05
MASK_FILL = -1e30


def shifted(block, axis, distance):
    devices = range(lax.axis_size(axis))
    route = [(i - distance, i) for i in devices if i - distance in devices]
    return lax.ppermute(block, axis, route)


def span_starts(seq_lens):
    span_counts = (seq_lens + SPAN - 1) // SPAN
    return jnp.cumsum(span_counts, dtype=jnp.int32) - span_counts


def token_layout(seq_lens, first_row, row_count):
    span_begin = span_starts(seq_lens)
    return layout_of(seq_lens, first_row + jnp.arange(row_count, dtype=jnp.int32), span_begin)


def layout_of(seq_lens, row_index, span_begin):
    row_span = row_index // SPAN
    row_doc = jnp.sum(
        (row_span[:, None] >= span_begin[None, 1:]).astype(jnp.int32), axis=1, dtype=jnp.int32
    )
    doc_onehot = row_doc[:, None] == jnp.arange(DOCS, dtype=jnp.int32)[None, :]
    doc_start = (
        jnp.sum(jnp.where(doc_onehot, span_begin[None, :], 0), axis=1, dtype=jnp.int32) * SPAN
    )
    doc_length = jnp.sum(jnp.where(doc_onehot, seq_lens[None, :], 0), axis=1, dtype=jnp.int32)
    row_pos = row_index - doc_start
    return (row_index, row_doc, row_pos, row_pos < doc_length)


def apply_rotary(values, positions, direction):
    half_dim = values.shape[-1] // 2
    frequency = 10000.0 ** (-jnp.arange(half_dim, dtype=jnp.float32) / half_dim)
    angles = positions.astype(jnp.float32)[:, None] * frequency[None, :]
    cosine = jnp.cos(angles)[:, None, :]
    sine_dir = direction * jnp.sin(angles)[:, None, :]
    leading = values[..., :half_dim]
    trailing = values[..., half_dim:]
    return jnp.concatenate(
        [leading * cosine - trailing * sine_dir, leading * sine_dir + trailing * cosine], axis=-1
    )


def times_transposed(left_mat, right_mat):
    return lax.dot_general(
        left_mat, right_mat, (((1,), (1,)), ((), ())), preferred_element_type=jnp.float32
    )


def transposed_times(left_mat, right_mat):
    return lax.dot_general(
        left_mat, right_mat, (((0,), (0,)), ((), ())), preferred_element_type=jnp.float32
    )


def norm_back(grad_out, normed, inv_scale, gain_vec):
    scaled = grad_out * gain_vec
    grad_gain = jnp.sum(grad_out * normed, axis=0)
    grad_values = inv_scale * (scaled - normed * jnp.mean(scaled * normed, axis=-1, keepdims=True))
    return (grad_gain, grad_values)


def tap_masks(positions):
    return [(positions >= lag).astype(jnp.float32)[:, None] for lag in range(CONV)]


def conv_forward(extended, kernel_f, bias_f, masks, row_count):
    total = bias_f[None, :] + jnp.zeros((row_count, extended.shape[1]), jnp.float32)
    for tap_no in range(CONV):
        total = (
            total
            + kernel_f[tap_no][None, :]
            * extended[tap_no : tap_no + row_count]
            * masks[CONV - 1 - tap_no]
        )
    return total


def conv_backward(grad_ext, extended, kernel_f, masks_ext, row_count):
    grad_values = jnp.zeros((row_count, grad_ext.shape[1]), jnp.float32)
    kernel_rows = []
    for tap_no in range(CONV):
        lag = CONV - 1 - tap_no
        masked = grad_ext * masks_ext[lag]
        grad_values = grad_values + kernel_f[tap_no][None, :] * masked[lag : lag + row_count]
        kernel_rows.append(
            jnp.sum(masked[:row_count] * extended[tap_no : tap_no + row_count], axis=0)
        )
    return (grad_values, jnp.stack(kernel_rows), jnp.sum(grad_ext[:row_count], axis=0))


def mamba_local(
    inner,
    states_in,
    intersection,
    step_raw,
    step_bias,
    decay_log,
    skip_gain,
    valid_float,
    span_keep,
    carry_in,
):
    row_total = inner.shape[0]
    head_count = step_raw.shape[1]
    span_total = row_total // SPAN
    step_size = jax.nn.softplus(step_raw + step_bias[None, :]) * valid_float[:, None]
    log_decay = -jnp.exp(decay_log)[None, :] * step_size
    inner_c = inner.reshape(span_total, SPAN, head_count, HEAD_DIM)
    b_mat = states_in[:, :STATE].reshape(span_total, SPAN, STATE)
    c_mat = states_in[:, STATE:].reshape(span_total, SPAN, STATE)
    step_c = step_size.reshape(span_total, SPAN, head_count)
    cumul = jnp.cumsum(log_decay.reshape(span_total, SPAN, head_count), axis=1)
    span_tail = cumul[:, -1]
    weights_in = jnp.exp(span_tail[:, None, :] - cumul) * step_c
    span_state = jnp.einsum(
        "cqh,cqn,cqhp->chnp", weights_in, b_mat, inner_c
    )
    entering = []
    running = carry_in
    for span_no in range(span_total):
        running = running * span_keep[span_no]
        entering.append(running)
        running = jnp.exp(span_tail[span_no])[:, None, None] * running + span_state[span_no]
    entering = jnp.stack(entering)
    inflow = jnp.exp(cumul)[..., None] * jnp.einsum(
        "cqn,chnp->cqhp", c_mat, entering
    )
    lower = jnp.arange(SPAN)[:, None] >= jnp.arange(SPAN)[None, :]
    gaps = cumul[:, :, None, :] - cumul[:, None, :, :]
    decay_mat = jnp.exp(jnp.where(lower[None, :, :, None], gaps, MASK_FILL))
    mixing = decay_mat * intersection[..., None] * step_c[:, None, :, :]
    within = jnp.einsum("cqkh,ckhp->cqhp", mixing, inner_c)
    result = (inflow + within + skip_gain[None, None, :, None] * inner_c).reshape(
        row_total, head_count * HEAD_DIM
    )
    total_decay = jnp.prod(span_keep[:, None] * jnp.exp(span_tail), axis=0)
    return (result, total_decay, running)


def tensor_sum(values):
    low = values.astype(jnp.bfloat16)
    if lax.axis_size("tp") != 2:
        return lax.psum(low, "tp").astype(jnp.float32)
    other = lax.ppermute(low, "tp", [(0, 1), (1, 0)])
    return low.astype(jnp.float32) + other.astype(jnp.float32)


def gather_state(state, decay):
    high = decay.astype(jnp.bfloat16)
    rest = (decay - high.astype(jnp.float32)).astype(jnp.bfloat16)
    heads, _, width = state.shape
    extra = jnp.stack([high, rest] + [jnp.zeros_like(high)] * 6, axis=1)
    extra = jnp.broadcast_to(extra[:, :, None], (heads, 8, width))
    packed = jnp.concatenate([state.astype(jnp.bfloat16), extra], axis=1)
    every = lax.all_gather(packed, "ctx", axis=0, tiled=False).astype(jnp.float32)
    return every[:, :, :STATE], every[:, :, STATE, 0] + every[:, :, STATE + 1, 0]


def local(
    hidden_in,
    cotangent,
    lengths,
    first_gain,
    second_gain,
    mamba_gate,
    mamba_inner,
    mamba_step,
    mamba_states,
    query_weight,
    keyval_weight,
    mamba_output,
    attention_output,
    gate_weight,
    up_weight,
    down_weight,
    decay_log,
    step_bias,
    skip_gain,
    conv_inner,
    conv_inner_bias,
    conv_states,
    conv_states_bias,
):
    both = ("shard", "ctx")
    shard_rows = mamba_gate.shape[0]
    inner_w = mamba_inner.shape[1]
    q_width = query_weight.shape[1]
    kv_width = keyval_weight.shape[1]
    head_local = mamba_step.shape[1]
    ff_w = gate_weight.shape[1]
    at_query = 2 * inner_w
    at_keyval = at_query + q_width
    at_small = at_keyval + kv_width
    at_states = at_small + 128
    small_cols = jnp.concatenate(
        [
            mamba_step,
            first_gain[:, None],
            second_gain[:, None],
            jnp.zeros((shard_rows, 128 - head_local - 2), jnp.bfloat16),
        ],
        axis=1,
    )
    mixer_shard = jnp.concatenate(
        [mamba_gate, mamba_inner, query_weight, keyval_weight, small_cols, mamba_states], axis=1
    )
    later_shard = jnp.concatenate(
        [gate_weight, up_weight, down_weight.T, attention_output.T, mamba_output.T], axis=1
    )
    mixer_w = lax.all_gather(mixer_shard, both, axis=0, tiled=True)
    mixer_w, later_shard = lax.optimization_barrier((mixer_w, later_shard))
    later_w = lax.all_gather(later_shard, both, axis=0, tiled=True)
    gate_up = later_w[:, : 2 * ff_w]
    down_t = later_w[:, 2 * ff_w : 3 * ff_w]
    out_t = later_w[:, 3 * ff_w :]
    small_w = mixer_w[:, at_small:at_states]
    states_w = mixer_w[:, at_states:]
    pick = (
        jnp.arange(8, dtype=jnp.int32)[:, None] + head_local
        == jnp.arange(128, dtype=jnp.int32)[None, :]
    ).astype(jnp.bfloat16)
    gains = times_transposed(pick, small_w)
    gain_one_f = gains[0]
    gain_two_f = gains[1]

    seq_lens = lengths[0]
    row_total, model_w = hidden_in.shape
    ctx_count = lax.axis_size("ctx")
    ctx_index = lax.axis_index("ctx")
    tp_index = lax.axis_index("tp")
    span_begin = span_starts(seq_lens)
    row_index, row_doc, row_pos, row_valid = token_layout(
        seq_lens, ctx_index * row_total, row_total
    )
    valid_float = row_valid.astype(jnp.float32)
    span_keep = (row_pos[::SPAN] != 0).astype(jnp.float32)
    hidden_f = hidden_in.astype(jnp.float32)
    inv_one = lax.rsqrt(jnp.mean(hidden_f * hidden_f, axis=-1, keepdims=True) + NORM_EPS)
    normed_one = hidden_f * inv_one
    mixer_in = (normed_one * gain_one_f).astype(jnp.bfloat16)
    q_heads = q_width // HEAD_DIM
    score_scale = HEAD_DIM ** (-0.5)
    lin = jnp.dot(mixer_in, mixer_w, preferred_element_type=jnp.float32)
    mgate_lin = lin[:, :inner_w]
    inner_pre = lin[:, inner_w:at_query].astype(jnp.bfloat16)
    query_lin = lin[:, at_query:at_keyval]
    keyval_lin = lin[:, at_keyval:at_small]
    step_raw = lin[:, at_small : at_small + head_local]
    states_pre = lin[:, at_states:].astype(jnp.bfloat16)
    lead_rows = CONV - 1
    halo = shifted(
        jnp.concatenate(
            [inner_pre[row_total - lead_rows :], states_pre[row_total - lead_rows :]], axis=1
        ),
        "ctx",
        1,
    )
    query_rot = apply_rotary(query_lin.reshape(row_total, q_heads, HEAD_DIM), row_pos, 1.0).astype(
        jnp.bfloat16
    )
    key_rot = apply_rotary(keyval_lin[:, None, :HEAD_DIM], row_pos, 1.0)[:, 0]
    key_send = jnp.concatenate([key_rot, keyval_lin[:, HEAD_DIM:]], axis=1).astype(jnp.bfloat16)
    direct_keys = ctx_count <= 4
    if direct_keys:
        step_rows = ctx_count * row_total
        key_all = jnp.concatenate(
            [key_send] + [shifted(key_send, "ctx", back) for back in range(1, ctx_count)], axis=0
        )
        key_numbers = jnp.concatenate(
            [
                (ctx_index - back) * row_total + jnp.arange(row_total, dtype=jnp.int32)
                for back in range(ctx_count)
            ]
        )
    else:
        key_all = lax.all_gather(key_send, "ctx", axis=0, tiled=True)
        step_rows = row_total * 4 if ctx_count % 4 == 0 else row_total
        key_numbers = jnp.arange(ctx_count * row_total, dtype=jnp.int32)
    key_blocks = key_all.reshape(-1, step_rows, kv_width)
    key_numbers = key_numbers.reshape(-1, step_rows)

    def allowed_pairs(key_number):
        key_index, key_doc, _, key_valid = layout_of(seq_lens, key_number, span_begin)
        return (
            (key_doc[None, :] == row_doc[:, None])
            & (key_index[None, :] <= row_index[:, None])
            & (key_valid & (key_index >= 0))[None, :]
        )

    def attend_block(carried, block_in):
        block_keys, key_number = block_in
        run_max, run_sum, run_acc = carried
        allowed = allowed_pairs(key_number)
        scores = (
            jnp.einsum(
                "qhd,kd->qhk",
                query_rot,
                block_keys[:, :HEAD_DIM],
                preferred_element_type=jnp.float32,
            )
            * score_scale
        )
        scores = jnp.where(allowed[:, None, :], scores, MASK_FILL)
        new_max = jnp.maximum(run_max, jnp.max(scores, axis=-1))
        probs = jnp.where(allowed[:, None, :], jnp.exp(scores - new_max[..., None]), 0.0)
        factor = jnp.exp(run_max - new_max)
        run_sum = run_sum * factor + jnp.sum(probs, axis=-1)
        run_acc = run_acc * factor[..., None] + jnp.einsum(
            "qhk,kd->qhd",
            probs.astype(jnp.bfloat16),
            block_keys[:, HEAD_DIM:],
            preferred_element_type=jnp.float32,
        )
        return ((new_max, run_sum, run_acc), None)

    start_fold = (
        jnp.full((row_total, q_heads), MASK_FILL, jnp.float32),
        jnp.zeros((row_total, q_heads), jnp.float32),
        jnp.zeros((row_total, q_heads, HEAD_DIM), jnp.float32),
    )
    if direct_keys:
        (run_max, run_sum, run_acc), _ = attend_block(start_fold, (key_blocks[0], key_numbers[0]))
    else:
        (run_max, run_sum, run_acc), _ = lax.scan(
            attend_block, start_fold, (key_blocks, key_numbers)
        )
    attn_heads = run_acc / run_sum[..., None]
    log_total = run_max + jnp.log(run_sum)
    attn_low = attn_heads.reshape(row_total, -1).astype(jnp.bfloat16)

    inner_ext = jnp.concatenate([halo[:, :inner_w], inner_pre], axis=0).astype(jnp.float32)
    states_ext = jnp.concatenate([halo[:, inner_w:], states_pre], axis=0).astype(jnp.float32)
    own_masks = tap_masks(row_pos)
    conv_in_w = conv_inner.astype(jnp.float32)
    conv_st_w = conv_states.astype(jnp.float32)
    inner_conv = conv_forward(
        inner_ext, conv_in_w, conv_inner_bias.astype(jnp.float32), own_masks, row_total
    )
    states_conv = conv_forward(
        states_ext, conv_st_w, conv_states_bias.astype(jnp.float32), own_masks, row_total
    )
    sig_inner = jax.nn.sigmoid(inner_conv)
    sig_states = jax.nn.sigmoid(states_conv)
    inner_low = (inner_conv * sig_inner).astype(jnp.bfloat16)
    states_low = (states_conv * sig_states).astype(jnp.bfloat16)
    inner_f = inner_low.astype(jnp.float32)
    states_f = states_low.astype(jnp.float32)
    span_total = row_total // SPAN
    b_low = states_low[:, :STATE].reshape(span_total, SPAN, STATE)
    c_low = states_low[:, STATE:].reshape(span_total, SPAN, STATE)
    intersection = jnp.einsum("cqn,ckn->cqk", c_low, b_low, preferred_element_type=jnp.float32)

    def mamba_fn(
        inner_arg, states_arg, intersection_arg, raw_arg, bias_arg, decay_arg, skip_arg, carry_arg
    ):
        return mamba_local(
            inner_arg,
            states_arg,
            intersection_arg,
            raw_arg,
            bias_arg,
            decay_arg,
            skip_arg,
            valid_float,
            span_keep,
            carry_arg,
        )

    zero_carry = jnp.zeros((head_local, STATE, HEAD_DIM), jnp.float32)
    _, dev_decay, dev_state = mamba_fn(
        inner_f, states_f, intersection, step_raw, step_bias, decay_log, skip_gain, zero_carry
    )
    every_state, every_decay = gather_state(dev_state, dev_decay)
    carry_in = zero_carry
    for owner in range(ctx_count - 1):
        carry_in = jnp.where(
            owner < ctx_index,
            every_decay[owner][:, None, None] * carry_in + every_state[owner],
            carry_in,
        )
    mamba_y, _, _ = mamba_fn(
        inner_f, states_f, intersection, step_raw, step_bias, decay_log, skip_gain, carry_in
    )
    sig_mgate = jax.nn.sigmoid(mgate_lin)
    silu_mgate = mgate_lin * sig_mgate
    gated_low = (mamba_y * silu_mgate).astype(jnp.bfloat16)
    mixed_low = jnp.concatenate([attn_low, gated_low], axis=1)
    resid = hidden_f + tensor_sum(times_transposed(mixed_low, out_t))
    inv_two = lax.rsqrt(jnp.mean(resid * resid, axis=-1, keepdims=True) + NORM_EPS)
    normed_two = resid * inv_two
    ffn_in = (normed_two * gain_two_f).astype(jnp.bfloat16)
    gate_upper = jnp.dot(ffn_in, gate_up, preferred_element_type=jnp.float32)
    gate_lin = gate_upper[:, :ff_w]
    upper_lin = gate_upper[:, ff_w:]
    sig_ffn = jax.nn.sigmoid(gate_lin)
    silu_ffn = gate_lin * sig_ffn
    act_low = (silu_ffn * upper_lin).astype(jnp.bfloat16)
    output = resid + tensor_sum(times_transposed(act_low, down_t))
    cot_f = cotangent.astype(jnp.float32)
    dact = jnp.dot(cotangent, down_t, preferred_element_type=jnp.float32)
    dgate = (dact * upper_lin * sig_ffn * (1.0 + gate_lin * (1.0 - sig_ffn))).astype(jnp.bfloat16)
    dupper = (dact * silu_ffn).astype(jnp.bfloat16)
    dgate_upper = jnp.concatenate([dgate, dupper], axis=1)
    dffn_in = tensor_sum(times_transposed(dgate_upper, gate_up))
    grad_gain_two, dresid_norm = norm_back(dffn_in, normed_two, inv_two, gain_two_f)
    dresid = cot_f + dresid_norm
    dmix_low = dresid.astype(jnp.bfloat16)
    later_grad = jnp.concatenate(
        [
            transposed_times(ffn_in, dgate_upper).astype(jnp.bfloat16),
            transposed_times(cotangent, act_low).astype(jnp.bfloat16),
            transposed_times(dmix_low, mixed_low).astype(jnp.bfloat16),
        ],
        axis=1,
    )
    later_own = lax.psum_scatter(later_grad, both, scatter_dimension=0, tiled=True)
    dmixed = jnp.dot(dmix_low, out_t, preferred_element_type=jnp.float32)
    dattn = dmixed[:, :q_width].astype(jnp.bfloat16)
    dgated = dmixed[:, q_width:]
    dattn_heads = dattn.reshape(row_total, q_heads, HEAD_DIM)
    delta_rows = jnp.sum(dattn_heads.astype(jnp.float32) * attn_heads, axis=-1)

    def back_block(dq_acc, block_in):
        block_keys, key_number = block_in
        allowed = allowed_pairs(key_number)
        scores = (
            jnp.einsum(
                "qhd,kd->qhk",
                query_rot,
                block_keys[:, :HEAD_DIM],
                preferred_element_type=jnp.float32,
            )
            * score_scale
        )
        probs = jnp.where(allowed[:, None, :], jnp.exp(scores - log_total[..., None]), 0.0)
        dprobs = jnp.einsum(
            "qhd,kd->qhk", dattn_heads, block_keys[:, HEAD_DIM:], preferred_element_type=jnp.float32
        )
        dscore = (probs * (dprobs - delta_rows[..., None])).astype(jnp.bfloat16)
        dq_term = (
            jnp.einsum(
                "qhk,kd->qhd", dscore, block_keys[:, :HEAD_DIM], preferred_element_type=jnp.float32
            )
            * score_scale
        )
        dkey = (
            jnp.einsum("qhk,qhd->kd", dscore, query_rot, preferred_element_type=jnp.float32)
            * score_scale
        )
        dvalue = jnp.einsum(
            "qhk,qhd->kd",
            probs.astype(jnp.bfloat16),
            dattn_heads,
            preferred_element_type=jnp.float32,
        )
        return (dq_acc + dq_term, jnp.concatenate([dkey, dvalue], axis=1))

    dq_zero = jnp.zeros((row_total, q_heads, HEAD_DIM), jnp.float32)
    if direct_keys:
        dq_rot, dkv_terms = back_block(dq_zero, (key_blocks[0], key_numbers[0]))
        dkv_own = dkv_terms[:row_total]
        for back in range(1, ctx_count):
            term = dkv_terms[back * row_total : (back + 1) * row_total].astype(jnp.bfloat16)
            dkv_own = dkv_own + shifted(term, "ctx", -back).astype(jnp.float32)
    else:
        dq_rot, dkv_terms = lax.scan(back_block, dq_zero, (key_blocks, key_numbers))
        dkv_own = lax.psum_scatter(
            dkv_terms.reshape(-1, kv_width).astype(jnp.bfloat16),
            "ctx",
            scatter_dimension=0,
            tiled=True,
        ).astype(jnp.float32)
    dq_lin = apply_rotary(dq_rot, row_pos, -1.0).reshape(row_total, -1).astype(jnp.bfloat16)
    dkey_lin = apply_rotary(dkv_own[:, None, :HEAD_DIM], row_pos, -1.0)[:, 0]
    dkv_lin = jnp.concatenate([dkey_lin, dkv_own[:, HEAD_DIM:]], axis=1).astype(jnp.bfloat16)
    dmamba_y = dgated * silu_mgate
    dmgate = (dgated * mamba_y * sig_mgate * (1.0 + mgate_lin * (1.0 - sig_mgate))).astype(
        jnp.bfloat16
    )
    _, pull_carry = jax.vjp(
        lambda carry_arg: mamba_fn(
            inner_f, states_f, intersection, step_raw, step_bias, decay_log, skip_gain, carry_arg
        )[0],
        carry_in,
    )
    direct = pull_carry(dmamba_y)[0]
    every_direct = lax.all_gather(direct.astype(jnp.bfloat16), "ctx", axis=0, tiled=False).astype(
        jnp.float32
    )
    adjoint_next = zero_carry
    for owner in range(ctx_count - 1, 0, -1):
        adjoint_next = jnp.where(
            owner > ctx_index,
            every_decay[owner][:, None, None] * adjoint_next + every_direct[owner],
            adjoint_next,
        )
    _, pull_all = jax.vjp(
        mamba_fn,
        inner_f,
        states_f,
        intersection,
        step_raw,
        step_bias,
        decay_log,
        skip_gain,
        carry_in,
    )
    dinner, dstates_direct, doverlap, dstep_raw, dbias, ddecay, dskip, _ = pull_all(
        (dmamba_y, jnp.zeros_like(dev_decay), adjoint_next)
    )
    b_f = states_f[:, :STATE].reshape(span_total, SPAN, STATE)
    c_f = states_f[:, STATE:].reshape(span_total, SPAN, STATE)
    dc_over = jnp.einsum("cqk,ckn->cqn", doverlap, b_f).reshape(row_total, STATE)
    db_over = jnp.einsum("cqk,cqn->ckn", doverlap, c_f).reshape(row_total, STATE)
    dstates = dstates_direct + jnp.concatenate([db_over, dc_over], axis=1)
    grad_inner_conv = dinner * sig_inner * (1.0 + inner_conv * (1.0 - sig_inner))
    grad_states_conv = dstates * sig_states * (1.0 + states_conv * (1.0 - sig_states))
    next_rows = shifted(
        jnp.concatenate([grad_inner_conv[:lead_rows], grad_states_conv[:lead_rows]], axis=1),
        "ctx",
        -1,
    )
    next_pos = token_layout(seq_lens, (ctx_index + 1) * row_total, lead_rows)[2]
    ext_masks = tap_masks(jnp.concatenate([row_pos, next_pos], axis=0))
    dstates_pre, conv_states_part, conv_sbias_part = conv_backward(
        jnp.concatenate([grad_states_conv, next_rows[:, inner_w:]], axis=0),
        states_ext,
        conv_st_w,
        ext_masks,
        row_total,
    )
    states_sum = tensor_sum(
        jnp.concatenate(
            [
                dstates_pre,
                conv_states_part,
                conv_sbias_part[None],
                jnp.zeros((3, 2 * STATE), jnp.float32),
            ],
            axis=0,
        )
    )
    dstates_low = states_sum[:row_total].astype(jnp.bfloat16)
    conv_states_grad = states_sum[row_total : row_total + CONV]
    conv_sbias_grad = states_sum[row_total + CONV]
    dinner_pre, grad_conv_inner, grad_conv_inner_bias = conv_backward(
        jnp.concatenate([grad_inner_conv, next_rows[:, :inner_w]], axis=0),
        inner_ext,
        conv_in_w,
        ext_masks,
        row_total,
    )
    dinner_low = dinner_pre.astype(jnp.bfloat16)
    dstep_low = dstep_raw.astype(jnp.bfloat16)
    mine = tp_index == 0
    dstates_half = jnp.where(mine, dstates_low[:, :STATE], dstates_low[:, STATE:])
    states_half = jnp.where(mine, states_w[:, :STATE], states_w[:, STATE:])
    dlin = jnp.concatenate([dmgate, dinner_low, dq_lin, dkv_lin, dstates_half], axis=1)
    back_w = jnp.concatenate([mixer_w[:, :at_small], states_half], axis=1)
    mixer_grad = transposed_times(mixer_in, dlin).astype(jnp.bfloat16)
    mixer_own = lax.psum_scatter(mixer_grad, both, scatter_dimension=0, tiled=True)
    grad_step_t = transposed_times(dstep_low, mixer_in)
    dmixer_in = tensor_sum(
        times_transposed(dlin, back_w) + times_transposed(dstep_low, small_w[:, :head_local])
    )
    grad_gain_one, dhidden_norm = norm_back(dmixer_in, normed_one, inv_one, gain_one_f)
    grad_input = dresid + dhidden_norm

    def wide(rows):
        return jnp.pad(rows, ((0, 0), (0, model_w - rows.shape[1])))

    small = jnp.concatenate(
        [
            grad_step_t,
            grad_gain_one[None],
            grad_gain_two[None],
            wide(grad_conv_inner),
            wide(grad_conv_inner_bias[None]),
            conv_states_grad.reshape(1, -1),
            wide(conv_sbias_grad[None]),
            wide(jnp.concatenate([ddecay, dbias, dskip])[None]),
        ],
        axis=0,
    )
    spare = -small.shape[0] % 8
    small = lax.psum(jnp.pad(small, ((0, spare), (0, 0))), both)
    own_begin = (lax.axis_index("shard") * ctx_count + ctx_index) * shard_rows
    own_cols = lax.dynamic_slice_in_dim(small[: head_local + 2], own_begin, shard_rows, 1)
    base = head_local + 2
    conv_rows = small[base : base + CONV, :inner_w]
    conv_bias_row = small[base + CONV, :inner_w]
    cstates_row = small[base + CONV + 1].reshape(CONV, 2 * STATE)
    csbias_row = small[base + CONV + 2, : 2 * STATE]
    heads_row = small[base + CONV + 3]

    later_own = later_own.astype(jnp.float32)
    at_out = 3 * ff_w
    states_own = mixer_own[:, at_small : at_small + STATE]
    states_other = lax.ppermute(states_own, "tp", [(0, 1), (1, 0)])
    grad_states = jnp.where(
        mine,
        jnp.concatenate([states_own, states_other], axis=1),
        jnp.concatenate([states_other, states_own], axis=1),
    ).astype(jnp.float32)
    mixer_own = mixer_own.astype(jnp.float32)
    return (
        output,
        grad_input,
        own_cols[head_local],
        own_cols[head_local + 1],
        mixer_own[:, :inner_w],
        mixer_own[:, inner_w:at_query],
        own_cols[:head_local].T,
        grad_states,
        mixer_own[:, at_query:at_keyval],
        mixer_own[:, at_keyval:at_small],
        later_own[:, at_out + q_width :].T,
        later_own[:, at_out : at_out + q_width].T,
        later_own[:, :ff_w],
        later_own[:, ff_w : 2 * ff_w],
        later_own[:, 2 * ff_w : at_out].T,
        heads_row[:head_local],
        heads_row[head_local : 2 * head_local],
        heads_row[2 * head_local : 3 * head_local],
        conv_rows,
        conv_bias_row,
        cstates_row,
        csbias_row,
    )


def solution(mesh):
    in_specs = (
        P(("shard", "ctx"), None),
        P(("shard", "ctx"), None),
        P("shard", None),
        P(("shard", "ctx")),
        P(("shard", "ctx")),
        P(("shard", "ctx"), "tp"),
        P(("shard", "ctx"), "tp"),
        P(("shard", "ctx"), "tp"),
        P(("shard", "ctx"), None),
        P(("shard", "ctx"), "tp"),
        P(("shard", "ctx"), "tp"),
        P("tp", ("shard", "ctx")),
        P("tp", ("shard", "ctx")),
        P(("shard", "ctx"), "tp"),
        P(("shard", "ctx"), "tp"),
        P("tp", ("shard", "ctx")),
        P("tp"),
        P("tp"),
        P("tp"),
        P(None, "tp"),
        P("tp"),
        P(),
        P(),
    )
    out_specs = (
        P(("shard", "ctx"), None),
        P(("shard", "ctx"), None),
        P(("shard", "ctx")),
        P(("shard", "ctx")),
        P(("shard", "ctx"), "tp"),
        P(("shard", "ctx"), "tp"),
        P(("shard", "ctx"), "tp"),
        P(("shard", "ctx"), None),
        P(("shard", "ctx"), "tp"),
        P(("shard", "ctx"), "tp"),
        P("tp", ("shard", "ctx")),
        P("tp", ("shard", "ctx")),
        P(("shard", "ctx"), "tp"),
        P(("shard", "ctx"), "tp"),
        P("tp", ("shard", "ctx")),
        P("tp"),
        P("tp"),
        P("tp"),
        P(None, "tp"),
        P("tp"),
        P(),
        P(),
    )
    return jax.shard_map(local, mesh=mesh, in_specs=in_specs, out_specs=out_specs, check_vma=False)
```

```python
import jax
import jax.numpy as jnp
from jax import lax
from jax.sharding import PartitionSpec as P

HEAD_DIM = 64
STATE = 128
SPAN = 256
CONV = 4
DOCS = 3


NORM_EPS = 1e-05
MASK_FILL = -1e30


def shifted(block, axis, distance):
    devices = range(lax.axis_size(axis))
    route = [(i - distance, i) for i in devices if i - distance in devices]
    return lax.ppermute(block, axis, route)


def span_starts(seq_lens):
    span_counts = (seq_lens + SPAN - 1) // SPAN
    return jnp.cumsum(span_counts, dtype=jnp.int32) - span_counts


def token_layout(seq_lens, first_row, row_count):
    span_begin = span_starts(seq_lens)
    return layout_of(seq_lens, first_row + jnp.arange(row_count, dtype=jnp.int32), span_begin)


def layout_of(seq_lens, row_index, span_begin):
    row_span = row_index // SPAN
    row_doc = jnp.sum(
        (row_span[:, None] >= span_begin[None, 1:]).astype(jnp.int32), axis=1, dtype=jnp.int32
    )
    doc_onehot = row_doc[:, None] == jnp.arange(DOCS, dtype=jnp.int32)[None, :]
    doc_start = (
        jnp.sum(jnp.where(doc_onehot, span_begin[None, :], 0), axis=1, dtype=jnp.int32) * SPAN
    )
    doc_length = jnp.sum(jnp.where(doc_onehot, seq_lens[None, :], 0), axis=1, dtype=jnp.int32)
    row_pos = row_index - doc_start
    return (row_index, row_doc, row_pos, row_pos < doc_length)


def apply_rotary(values, positions, direction):
    half_dim = values.shape[-1] // 2
    frequency = 10000.0 ** (-jnp.arange(half_dim, dtype=jnp.float32) / half_dim)
    angles = positions.astype(jnp.float32)[:, None] * frequency[None, :]
    cosine = jnp.cos(angles)[:, None, :]
    sine_dir = direction * jnp.sin(angles)[:, None, :]
    leading = values[..., :half_dim]
    trailing = values[..., half_dim:]
    return jnp.concatenate(
        [leading * cosine - trailing * sine_dir, leading * sine_dir + trailing * cosine], axis=-1
    )


def times_transposed(left_mat, right_mat):
    return lax.dot_general(
        left_mat, right_mat, (((1,), (1,)), ((), ())), preferred_element_type=jnp.float32
    )


def transposed_times(left_mat, right_mat):
    return lax.dot_general(
        left_mat, right_mat, (((0,), (0,)), ((), ())), preferred_element_type=jnp.float32
    )


def norm_back(grad_out, normed, inv_scale, gain_vec):
    scaled = grad_out * gain_vec
    grad_gain = jnp.sum(grad_out * normed, axis=0)
    grad_values = inv_scale * (scaled - normed * jnp.mean(scaled * normed, axis=-1, keepdims=True))
    return (grad_gain, grad_values)


def tap_masks(positions):
    return [(positions >= lag).astype(jnp.float32)[:, None] for lag in range(CONV)]


def conv_forward(extended, kernel_f, bias_f, masks, row_count):
    total = bias_f[None, :] + jnp.zeros((row_count, extended.shape[1]), jnp.float32)
    for tap_no in range(CONV):
        total = (
            total
            + kernel_f[tap_no][None, :]
            * extended[tap_no : tap_no + row_count]
            * masks[CONV - 1 - tap_no]
        )
    return total


def conv_backward(grad_ext, extended, kernel_f, masks_ext, row_count):
    grad_values = jnp.zeros((row_count, grad_ext.shape[1]), jnp.float32)
    kernel_rows = []
    for tap_no in range(CONV):
        lag = CONV - 1 - tap_no
        masked = grad_ext * masks_ext[lag]
        grad_values = grad_values + kernel_f[tap_no][None, :] * masked[lag : lag + row_count]
        kernel_rows.append(
            jnp.sum(masked[:row_count] * extended[tap_no : tap_no + row_count], axis=0)
        )
    return (grad_values, jnp.stack(kernel_rows), jnp.sum(grad_ext[:row_count], axis=0))


def mamba_local(
    inner,
    states_in,
    intersection,
    step_raw,
    step_bias,
    decay_log,
    skip_gain,
    valid_float,
    span_keep,
    carry_in,
):
    row_total = inner.shape[0]
    head_count = step_raw.shape[1]
    span_total = row_total // SPAN
    step_size = jax.nn.softplus(step_raw + step_bias[None, :]) * valid_float[:, None]
    log_decay = -jnp.exp(decay_log)[None, :] * step_size
    inner_c = inner.reshape(span_total, SPAN, head_count, HEAD_DIM)
    b_mat = states_in[:, :STATE].reshape(span_total, SPAN, STATE)
    c_mat = states_in[:, STATE:].reshape(span_total, SPAN, STATE)
    step_c = step_size.reshape(span_total, SPAN, head_count)
    cumul = jnp.cumsum(log_decay.reshape(span_total, SPAN, head_count), axis=1)
    span_tail = cumul[:, -1]
    weights_in = jnp.exp(span_tail[:, None, :] - cumul) * step_c
    span_state = jnp.einsum(
        "cqh,cqn,cqhp->chnp", weights_in, b_mat, inner_c
    )
    entering = []
    running = carry_in
    for span_no in range(span_total):
        running = running * span_keep[span_no]
        entering.append(running)
        running = jnp.exp(span_tail[span_no])[:, None, None] * running + span_state[span_no]
    entering = jnp.stack(entering)
    inflow = jnp.exp(cumul)[..., None] * jnp.einsum(
        "cqn,chnp->cqhp", c_mat, entering
    )
    lower = jnp.arange(SPAN)[:, None] >= jnp.arange(SPAN)[None, :]
    gaps = cumul[:, :, None, :] - cumul[:, None, :, :]
    decay_mat = jnp.exp(jnp.where(lower[None, :, :, None], gaps, MASK_FILL))
    mixing = decay_mat * intersection[..., None] * step_c[:, None, :, :]
    within = jnp.einsum("cqkh,ckhp->cqhp", mixing, inner_c)
    result = (inflow + within + skip_gain[None, None, :, None] * inner_c).reshape(
        row_total, head_count * HEAD_DIM
    )
    total_decay = jnp.prod(span_keep[:, None] * jnp.exp(span_tail), axis=0)
    return (result, total_decay, running)


def tensor_sum(values):
    low = values.astype(jnp.bfloat16)
    if lax.axis_size("tp") != 2:
        return lax.psum(low, "tp").astype(jnp.float32)
    other = lax.ppermute(low, "tp", [(0, 1), (1, 0)])
    return low.astype(jnp.float32) + other.astype(jnp.float32)


def far_states(state, decay, direction):
    heads, _, width = state.shape
    high = decay.astype(jnp.bfloat16)
    rest = (decay - high.astype(jnp.float32)).astype(jnp.bfloat16)
    extra = jnp.stack([high, rest] + [jnp.zeros_like(high)] * 6, axis=1)
    extra = jnp.broadcast_to(extra[:, :, None], (heads, 8, width))
    packed = jnp.concatenate([state.astype(jnp.bfloat16), extra], axis=1)
    count = lax.axis_size("ctx")
    total = jnp.zeros(state.shape, jnp.float32)
    if count <= 4:
        for distance in range(count - 1, 0, -1):
            got = shifted(packed, "ctx", direction * distance).astype(jnp.float32)
            factor = got[:, STATE, 0] + got[:, STATE + 1, 0]
            total = factor[:, None, None] * total + got[:, :STATE]
        return total
    index = lax.axis_index("ctx")
    every = lax.all_gather(packed, "ctx", axis=0, tiled=False).astype(jnp.float32)
    for owner in range(count)[::direction]:
        factor = every[owner, :, STATE, 0] + every[owner, :, STATE + 1, 0]
        total = jnp.where(
            (index - owner) * direction > 0,
            factor[:, None, None] * total + every[owner, :, :STATE],
            total,
        )
    return total


def doubling_sum(values, axis):
    count = lax.axis_size(axis)
    if count & (count - 1):
        return lax.psum(values, axis)
    step = 1
    while step < count:
        values = values + lax.ppermute(values, axis, [(i, i ^ step) for i in range(count)])
        step = step * 2
    return values


def local(
    hidden_in,
    cotangent,
    lengths,
    first_gain,
    second_gain,
    mamba_gate,
    mamba_inner,
    mamba_step,
    mamba_states,
    query_weight,
    keyval_weight,
    mamba_output,
    attention_output,
    gate_weight,
    up_weight,
    down_weight,
    decay_log,
    step_bias,
    skip_gain,
    conv_inner,
    conv_inner_bias,
    conv_states,
    conv_states_bias,
):
    both = ("shard", "ctx")
    shard_rows = mamba_gate.shape[0]
    inner_w = mamba_inner.shape[1]
    q_width = query_weight.shape[1]
    kv_width = keyval_weight.shape[1]
    head_local = mamba_step.shape[1]
    ff_w = gate_weight.shape[1]
    at_states = inner_w
    at_keyval = at_states + 2 * STATE
    at_small = at_keyval + kv_width
    small_cols = jnp.concatenate(
        [
            mamba_step,
            first_gain[:, None],
            second_gain[:, None],
            jnp.zeros((shard_rows, 128 - head_local - 2), jnp.bfloat16),
        ],
        axis=1,
    )
    first_shard = jnp.concatenate([mamba_inner, mamba_states, keyval_weight, small_cols], axis=1)
    next_shard = jnp.concatenate(
        [attention_output.T, mamba_output.T, mamba_gate, query_weight], axis=1
    )
    last_shard = jnp.concatenate([gate_weight, up_weight, down_weight.T], axis=1)
    first_w = lax.all_gather(first_shard, both, axis=0, tiled=True)
    first_w, next_shard = lax.optimization_barrier((first_w, next_shard))
    next_w = lax.all_gather(next_shard, both, axis=0, tiled=True)
    next_w, last_shard = lax.optimization_barrier((next_w, last_shard))
    last_w = lax.all_gather(last_shard, both, axis=0, tiled=True)
    gate_up = last_w[:, : 2 * ff_w]
    down_t = last_w[:, 2 * ff_w :]
    at_gate = q_width + inner_w
    out_t = next_w[:, :at_gate]
    gate_query_w = next_w[:, at_gate:]
    small_w = first_w[:, at_small:]
    states_w = first_w[:, at_states:at_keyval]
    pick = (
        jnp.arange(8, dtype=jnp.int32)[:, None] + head_local
        == jnp.arange(128, dtype=jnp.int32)[None, :]
    ).astype(jnp.bfloat16)
    gains = times_transposed(pick, small_w)
    gain_one_f = gains[0]
    gain_two_f = gains[1]

    seq_lens = lengths[0]
    row_total, model_w = hidden_in.shape
    ctx_count = lax.axis_size("ctx")
    ctx_index = lax.axis_index("ctx")
    tp_index = lax.axis_index("tp")
    span_begin = span_starts(seq_lens)
    row_index, row_doc, row_pos, row_valid = token_layout(
        seq_lens, ctx_index * row_total, row_total
    )
    valid_float = row_valid.astype(jnp.float32)
    span_keep = (row_pos[::SPAN] != 0).astype(jnp.float32)
    hidden_f = hidden_in.astype(jnp.float32)
    inv_one = lax.rsqrt(jnp.mean(hidden_f * hidden_f, axis=-1, keepdims=True) + NORM_EPS)
    normed_one = hidden_f * inv_one
    mixer_in = (normed_one * gain_one_f).astype(jnp.bfloat16)
    q_heads = q_width // HEAD_DIM
    score_scale = HEAD_DIM ** (-0.5)
    lin = jnp.dot(mixer_in, first_w, preferred_element_type=jnp.float32)
    inner_pre = lin[:, :inner_w].astype(jnp.bfloat16)
    states_pre = lin[:, at_states:at_keyval].astype(jnp.bfloat16)
    keyval_lin = lin[:, at_keyval:at_small]
    step_raw = lin[:, at_small : at_small + head_local]
    lin_two = jnp.dot(mixer_in, gate_query_w, preferred_element_type=jnp.float32)
    mgate_lin = lin_two[:, :inner_w]
    query_lin = lin_two[:, inner_w:]
    lead_rows = CONV - 1
    halo = shifted(
        jnp.concatenate(
            [inner_pre[row_total - lead_rows :], states_pre[row_total - lead_rows :]], axis=1
        ),
        "ctx",
        1,
    )
    query_rot = apply_rotary(query_lin.reshape(row_total, q_heads, HEAD_DIM), row_pos, 1.0).astype(
        jnp.bfloat16
    )
    key_rot = apply_rotary(keyval_lin[:, None, :HEAD_DIM], row_pos, 1.0)[:, 0]
    key_send = jnp.concatenate([key_rot, keyval_lin[:, HEAD_DIM:]], axis=1).astype(jnp.bfloat16)
    direct_keys = ctx_count <= 4
    if direct_keys:
        step_rows = ctx_count * row_total
        key_all = jnp.concatenate(
            [key_send] + [shifted(key_send, "ctx", back) for back in range(1, ctx_count)], axis=0
        )
        key_numbers = jnp.concatenate(
            [
                (ctx_index - back) * row_total + jnp.arange(row_total, dtype=jnp.int32)
                for back in range(ctx_count)
            ]
        )
    else:
        key_all = lax.all_gather(key_send, "ctx", axis=0, tiled=True)
        step_rows = row_total * 4 if ctx_count % 4 == 0 else row_total
        key_numbers = jnp.arange(ctx_count * row_total, dtype=jnp.int32)
    key_blocks = key_all.reshape(-1, step_rows, kv_width)
    key_numbers = key_numbers.reshape(-1, step_rows)

    def allowed_pairs(key_number):
        key_index, key_doc, _, key_valid = layout_of(seq_lens, key_number, span_begin)
        return (
            (key_doc[None, :] == row_doc[:, None])
            & (key_index[None, :] <= row_index[:, None])
            & (key_valid & (key_index >= 0))[None, :]
        )

    def attend_block(carried, block_in):
        block_keys, key_number = block_in
        run_max, run_sum, run_acc = carried
        allowed = allowed_pairs(key_number)
        scores = (
            jnp.einsum(
                "qhd,kd->qhk",
                query_rot,
                block_keys[:, :HEAD_DIM],
                preferred_element_type=jnp.float32,
            )
            * score_scale
        )
        scores = jnp.where(allowed[:, None, :], scores, MASK_FILL)
        new_max = jnp.maximum(run_max, jnp.max(scores, axis=-1))
        probs = jnp.where(allowed[:, None, :], jnp.exp(scores - new_max[..., None]), 0.0)
        factor = jnp.exp(run_max - new_max)
        run_sum = run_sum * factor + jnp.sum(probs, axis=-1)
        run_acc = run_acc * factor[..., None] + jnp.einsum(
            "qhk,kd->qhd",
            probs.astype(jnp.bfloat16),
            block_keys[:, HEAD_DIM:],
            preferred_element_type=jnp.float32,
        )
        return ((new_max, run_sum, run_acc), None)

    start_fold = (
        jnp.full((row_total, q_heads), MASK_FILL, jnp.float32),
        jnp.zeros((row_total, q_heads), jnp.float32),
        jnp.zeros((row_total, q_heads, HEAD_DIM), jnp.float32),
    )
    if direct_keys:
        (run_max, run_sum, run_acc), _ = attend_block(start_fold, (key_blocks[0], key_numbers[0]))
    else:
        (run_max, run_sum, run_acc), _ = lax.scan(
            attend_block, start_fold, (key_blocks, key_numbers)
        )
    attn_heads = run_acc / run_sum[..., None]
    log_total = run_max + jnp.log(run_sum)
    attn_low = attn_heads.reshape(row_total, -1).astype(jnp.bfloat16)

    inner_ext = jnp.concatenate([halo[:, :inner_w], inner_pre], axis=0).astype(jnp.float32)
    states_ext = jnp.concatenate([halo[:, inner_w:], states_pre], axis=0).astype(jnp.float32)
    own_masks = tap_masks(row_pos)
    conv_in_w = conv_inner.astype(jnp.float32)
    conv_st_w = conv_states.astype(jnp.float32)
    inner_conv = conv_forward(
        inner_ext, conv_in_w, conv_inner_bias.astype(jnp.float32), own_masks, row_total
    )
    states_conv = conv_forward(
        states_ext, conv_st_w, conv_states_bias.astype(jnp.float32), own_masks, row_total
    )
    sig_inner = jax.nn.sigmoid(inner_conv)
    sig_states = jax.nn.sigmoid(states_conv)
    inner_low = (inner_conv * sig_inner).astype(jnp.bfloat16)
    states_low = (states_conv * sig_states).astype(jnp.bfloat16)
    inner_f = inner_low.astype(jnp.float32)
    states_f = states_low.astype(jnp.float32)
    span_total = row_total // SPAN
    b_low = states_low[:, :STATE].reshape(span_total, SPAN, STATE)
    c_low = states_low[:, STATE:].reshape(span_total, SPAN, STATE)
    intersection = jnp.einsum("cqn,ckn->cqk", c_low, b_low, preferred_element_type=jnp.float32)

    def mamba_fn(
        inner_arg, states_arg, intersection_arg, raw_arg, bias_arg, decay_arg, skip_arg, carry_arg
    ):
        return mamba_local(
            inner_arg,
            states_arg,
            intersection_arg,
            raw_arg,
            bias_arg,
            decay_arg,
            skip_arg,
            valid_float,
            span_keep,
            carry_arg,
        )

    zero_carry = jnp.zeros((head_local, STATE, HEAD_DIM), jnp.float32)
    _, dev_decay, dev_state = mamba_fn(
        inner_f, states_f, intersection, step_raw, step_bias, decay_log, skip_gain, zero_carry
    )
    carry_in = far_states(dev_state, dev_decay, 1)
    mamba_y, _, _ = mamba_fn(
        inner_f, states_f, intersection, step_raw, step_bias, decay_log, skip_gain, carry_in
    )
    sig_mgate = jax.nn.sigmoid(mgate_lin)
    silu_mgate = mgate_lin * sig_mgate
    gated_low = (mamba_y * silu_mgate).astype(jnp.bfloat16)
    mixed_low = jnp.concatenate([attn_low, gated_low], axis=1)
    resid = hidden_f + tensor_sum(times_transposed(mixed_low, out_t))
    inv_two = lax.rsqrt(jnp.mean(resid * resid, axis=-1, keepdims=True) + NORM_EPS)
    normed_two = resid * inv_two
    ffn_in = (normed_two * gain_two_f).astype(jnp.bfloat16)
    gate_upper = jnp.dot(ffn_in, gate_up, preferred_element_type=jnp.float32)
    gate_lin = gate_upper[:, :ff_w]
    upper_lin = gate_upper[:, ff_w:]
    sig_ffn = jax.nn.sigmoid(gate_lin)
    silu_ffn = gate_lin * sig_ffn
    act_low = (silu_ffn * upper_lin).astype(jnp.bfloat16)
    output = resid + tensor_sum(times_transposed(act_low, down_t))
    cot_f = cotangent.astype(jnp.float32)
    dact = jnp.dot(cotangent, down_t, preferred_element_type=jnp.float32)
    dgate = (dact * upper_lin * sig_ffn * (1.0 + gate_lin * (1.0 - sig_ffn))).astype(jnp.bfloat16)
    dupper = (dact * silu_ffn).astype(jnp.bfloat16)
    dgate_upper = jnp.concatenate([dgate, dupper], axis=1)
    dffn_in = tensor_sum(times_transposed(dgate_upper, gate_up))
    last_grad = jnp.concatenate(
        [
            transposed_times(ffn_in, dgate_upper).astype(jnp.bfloat16),
            transposed_times(cotangent, act_low).astype(jnp.bfloat16),
        ],
        axis=1,
    )
    last_own = lax.psum_scatter(last_grad, both, scatter_dimension=0, tiled=True)
    grad_gain_two, dresid_norm = norm_back(dffn_in, normed_two, inv_two, gain_two_f)
    dresid = cot_f + dresid_norm
    dmix_low = dresid.astype(jnp.bfloat16)
    dmixed = jnp.dot(dmix_low, out_t, preferred_element_type=jnp.float32)
    dattn = dmixed[:, :q_width].astype(jnp.bfloat16)
    dgated = dmixed[:, q_width:]
    dattn_heads = dattn.reshape(row_total, q_heads, HEAD_DIM)
    delta_rows = jnp.sum(dattn_heads.astype(jnp.float32) * attn_heads, axis=-1)

    def back_block(dq_acc, block_in):
        block_keys, key_number = block_in
        allowed = allowed_pairs(key_number)
        scores = (
            jnp.einsum(
                "qhd,kd->qhk",
                query_rot,
                block_keys[:, :HEAD_DIM],
                preferred_element_type=jnp.float32,
            )
            * score_scale
        )
        probs = jnp.where(allowed[:, None, :], jnp.exp(scores - log_total[..., None]), 0.0)
        dprobs = jnp.einsum(
            "qhd,kd->qhk", dattn_heads, block_keys[:, HEAD_DIM:], preferred_element_type=jnp.float32
        )
        dscore = (probs * (dprobs - delta_rows[..., None])).astype(jnp.bfloat16)
        dq_term = (
            jnp.einsum(
                "qhk,kd->qhd", dscore, block_keys[:, :HEAD_DIM], preferred_element_type=jnp.float32
            )
            * score_scale
        )
        dkey = (
            jnp.einsum("qhk,qhd->kd", dscore, query_rot, preferred_element_type=jnp.float32)
            * score_scale
        )
        dvalue = jnp.einsum(
            "qhk,qhd->kd",
            probs.astype(jnp.bfloat16),
            dattn_heads,
            preferred_element_type=jnp.float32,
        )
        return (dq_acc + dq_term, jnp.concatenate([dkey, dvalue], axis=1))

    dq_zero = jnp.zeros((row_total, q_heads, HEAD_DIM), jnp.float32)
    if direct_keys:
        dq_rot, dkv_terms = back_block(dq_zero, (key_blocks[0], key_numbers[0]))
        dkv_own = dkv_terms[:row_total]
        for back in range(1, ctx_count):
            term = dkv_terms[back * row_total : (back + 1) * row_total].astype(jnp.bfloat16)
            dkv_own = dkv_own + shifted(term, "ctx", -back).astype(jnp.float32)
    else:
        dq_rot, dkv_terms = lax.scan(back_block, dq_zero, (key_blocks, key_numbers))
        dkv_own = lax.psum_scatter(
            dkv_terms.reshape(-1, kv_width).astype(jnp.bfloat16),
            "ctx",
            scatter_dimension=0,
            tiled=True,
        ).astype(jnp.float32)
    dq_lin = apply_rotary(dq_rot, row_pos, -1.0).reshape(row_total, -1).astype(jnp.bfloat16)
    dkey_lin = apply_rotary(dkv_own[:, None, :HEAD_DIM], row_pos, -1.0)[:, 0]
    dkv_lin = jnp.concatenate([dkey_lin, dkv_own[:, HEAD_DIM:]], axis=1).astype(jnp.bfloat16)
    dmamba_y = dgated * silu_mgate
    dmgate = (dgated * mamba_y * sig_mgate * (1.0 + mgate_lin * (1.0 - sig_mgate))).astype(
        jnp.bfloat16
    )
    dgate_query = jnp.concatenate([dmgate, dq_lin], axis=1)
    next_grad = jnp.concatenate(
        [
            transposed_times(dmix_low, mixed_low).astype(jnp.bfloat16),
            transposed_times(mixer_in, dgate_query).astype(jnp.bfloat16),
        ],
        axis=1,
    )
    next_grad, last_own = lax.optimization_barrier((next_grad, last_own))
    next_own = lax.psum_scatter(next_grad, both, scatter_dimension=0, tiled=True)
    _, pull_carry = jax.vjp(
        lambda carry_arg: mamba_fn(
            inner_f, states_f, intersection, step_raw, step_bias, decay_log, skip_gain, carry_arg
        )[0],
        carry_in,
    )
    direct = pull_carry(dmamba_y)[0]
    adjoint_next = far_states(direct, dev_decay, -1)
    _, pull_all = jax.vjp(
        mamba_fn,
        inner_f,
        states_f,
        intersection,
        step_raw,
        step_bias,
        decay_log,
        skip_gain,
        carry_in,
    )
    dinner, dstates_direct, doverlap, dstep_raw, dbias, ddecay, dskip, _ = pull_all(
        (dmamba_y, jnp.zeros_like(dev_decay), adjoint_next)
    )
    b_f = states_f[:, :STATE].reshape(span_total, SPAN, STATE)
    c_f = states_f[:, STATE:].reshape(span_total, SPAN, STATE)
    dc_over = jnp.einsum("cqk,ckn->cqn", doverlap, b_f).reshape(row_total, STATE)
    db_over = jnp.einsum("cqk,cqn->ckn", doverlap, c_f).reshape(row_total, STATE)
    dstates = dstates_direct + jnp.concatenate([db_over, dc_over], axis=1)
    grad_inner_conv = dinner * sig_inner * (1.0 + inner_conv * (1.0 - sig_inner))
    grad_states_conv = dstates * sig_states * (1.0 + states_conv * (1.0 - sig_states))
    next_rows = shifted(
        jnp.concatenate([grad_inner_conv[:lead_rows], grad_states_conv[:lead_rows]], axis=1),
        "ctx",
        -1,
    )
    next_pos = token_layout(seq_lens, (ctx_index + 1) * row_total, lead_rows)[2]
    ext_masks = tap_masks(jnp.concatenate([row_pos, next_pos], axis=0))
    dstates_pre, conv_states_part, conv_sbias_part = conv_backward(
        jnp.concatenate([grad_states_conv, next_rows[:, inner_w:]], axis=0),
        states_ext,
        conv_st_w,
        ext_masks,
        row_total,
    )
    states_sum = tensor_sum(
        jnp.concatenate(
            [
                dstates_pre,
                conv_states_part,
                conv_sbias_part[None],
                jnp.zeros((3, 2 * STATE), jnp.float32),
            ],
            axis=0,
        )
    )
    dstates_low = states_sum[:row_total].astype(jnp.bfloat16)
    conv_states_grad = states_sum[row_total : row_total + CONV]
    conv_sbias_grad = states_sum[row_total + CONV]
    dinner_pre, grad_conv_inner, grad_conv_inner_bias = conv_backward(
        jnp.concatenate([grad_inner_conv, next_rows[:, :inner_w]], axis=0),
        inner_ext,
        conv_in_w,
        ext_masks,
        row_total,
    )
    dinner_low = dinner_pre.astype(jnp.bfloat16)
    dstep_low = dstep_raw.astype(jnp.bfloat16)
    mine = tp_index == 0
    dstates_half = jnp.where(mine, dstates_low[:, :STATE], dstates_low[:, STATE:])
    states_half = jnp.where(mine, states_w[:, :STATE], states_w[:, STATE:])
    dlin = jnp.concatenate([dinner_low, dstates_half, dkv_lin], axis=1)
    back_w = jnp.concatenate([first_w[:, :inner_w], states_half, first_w[:, at_keyval:at_small]], axis=1)
    first_grad = transposed_times(mixer_in, dlin).astype(jnp.bfloat16)
    first_grad, next_own = lax.optimization_barrier((first_grad, next_own))
    first_own = lax.psum_scatter(first_grad, both, scatter_dimension=0, tiled=True)
    grad_step_t = transposed_times(dstep_low, mixer_in)
    dmixer_in = tensor_sum(
        times_transposed(dgate_query, gate_query_w)
        + times_transposed(dlin, back_w)
        + times_transposed(dstep_low, small_w[:, :head_local])
    )
    grad_gain_one, dhidden_norm = norm_back(dmixer_in, normed_one, inv_one, gain_one_f)
    grad_input = dresid + dhidden_norm

    def wide(rows):
        return jnp.pad(rows, ((0, 0), (0, model_w - rows.shape[1])))

    small = jnp.concatenate(
        [
            grad_step_t,
            grad_gain_one[None],
            grad_gain_two[None],
            wide(grad_conv_inner),
            wide(grad_conv_inner_bias[None]),
            conv_states_grad.reshape(1, -1),
            wide(conv_sbias_grad[None]),
            wide(jnp.concatenate([ddecay, dbias, dskip])[None]),
        ],
        axis=0,
    )
    spare = -small.shape[0] % 8
    small = doubling_sum(doubling_sum(jnp.pad(small, ((0, spare), (0, 0))), "shard"), "ctx")
    own_begin = (lax.axis_index("shard") * ctx_count + ctx_index) * shard_rows
    own_cols = lax.dynamic_slice_in_dim(small[: head_local + 2], own_begin, shard_rows, 1)
    base = head_local + 2
    conv_rows = small[base : base + CONV, :inner_w]
    conv_bias_row = small[base + CONV, :inner_w]
    cstates_row = small[base + CONV + 1].reshape(CONV, 2 * STATE)
    csbias_row = small[base + CONV + 2, : 2 * STATE]
    heads_row = small[base + CONV + 3]

    at_kv = inner_w + STATE
    states_own = first_own[:, inner_w:at_kv]
    states_other = lax.ppermute(states_own, "tp", [(0, 1), (1, 0)])
    grad_states = jnp.where(
        mine,
        jnp.concatenate([states_own, states_other], axis=1),
        jnp.concatenate([states_other, states_own], axis=1),
    ).astype(jnp.float32)
    first_own = first_own.astype(jnp.float32)
    next_own = next_own.astype(jnp.float32)
    last_own = last_own.astype(jnp.float32)
    return (
        output,
        grad_input,
        own_cols[head_local],
        own_cols[head_local + 1],
        next_own[:, at_gate : at_gate + inner_w],
        first_own[:, :inner_w],
        own_cols[:head_local].T,
        grad_states,
        next_own[:, at_gate + inner_w :],
        first_own[:, at_kv:],
        next_own[:, q_width:at_gate].T,
        next_own[:, :q_width].T,
        last_own[:, :ff_w],
        last_own[:, ff_w : 2 * ff_w],
        last_own[:, 2 * ff_w :].T,
        heads_row[:head_local],
        heads_row[head_local : 2 * head_local],
        heads_row[2 * head_local : 3 * head_local],
        conv_rows,
        conv_bias_row,
        cstates_row,
        csbias_row,
    )


def solution(mesh):
    in_specs = (
        P(("shard", "ctx"), None),
        P(("shard", "ctx"), None),
        P("shard", None),
        P(("shard", "ctx")),
        P(("shard", "ctx")),
        P(("shard", "ctx"), "tp"),
        P(("shard", "ctx"), "tp"),
        P(("shard", "ctx"), "tp"),
        P(("shard", "ctx"), None),
        P(("shard", "ctx"), "tp"),
        P(("shard", "ctx"), "tp"),
        P("tp", ("shard", "ctx")),
        P("tp", ("shard", "ctx")),
        P(("shard", "ctx"), "tp"),
        P(("shard", "ctx"), "tp"),
        P("tp", ("shard", "ctx")),
        P("tp"),
        P("tp"),
        P("tp"),
        P(None, "tp"),
        P("tp"),
        P(),
        P(),
    )
    out_specs = (
        P(("shard", "ctx"), None),
        P(("shard", "ctx"), None),
        P(("shard", "ctx")),
        P(("shard", "ctx")),
        P(("shard", "ctx"), "tp"),
        P(("shard", "ctx"), "tp"),
        P(("shard", "ctx"), "tp"),
        P(("shard", "ctx"), None),
        P(("shard", "ctx"), "tp"),
        P(("shard", "ctx"), "tp"),
        P("tp", ("shard", "ctx")),
        P("tp", ("shard", "ctx")),
        P(("shard", "ctx"), "tp"),
        P(("shard", "ctx"), "tp"),
        P("tp", ("shard", "ctx")),
        P("tp"),
        P("tp"),
        P("tp"),
        P(None, "tp"),
        P("tp"),
        P(),
        P(),
    )
    return jax.shard_map(local, mesh=mesh, in_specs=in_specs, out_specs=out_specs, check_vma=False)
```
